128 devices in a mesh: scene: 8 (over y, core), seg: 16 (over x, z).
Axes of the slice: x: 4, y: 4, z: 4, core: 2. Of those that a mesh axis runs over, the one named last changes fastest.
Arguments:
- points: bfloat16 [196608, 512], P(('scene', 'seg')), may hold values from -6 to 6
- zorder: int32 [1536], P(('scene', 'seg')), may hold values from 0 to 1535, as said below
- image: bfloat16 [16384, 1024], P(('scene', 'seg')), may hold values from -6 to 6
- image_row: int32 [196608], P(('scene', 'seg')), may hold values from 0 to 16383, as said below
- image_weight: bfloat16 [1024, 512], replicated, may hold values from -0.1875 to 0.1875
- norm_gain: float32 [2, 2, 512], replicated, may hold values from 0.1 to 1.9
- in_weight: bfloat16 [2, 512, 1536], replicated, may hold values from -16 to 16
- out_weight: bfloat16 [2, 512, 512], replicated, may hold values from -0.25 to 0.25
- up_weight: bfloat16 [2, 512, 2048], replicated, may hold values from -0.25 to 0.25
- down_weight: bfloat16 [2, 2048, 512], replicated, may hold values from -0.125 to 0.125
- hilbert_target: int32 [1536], P(('scene', 'seg')), may hold values from 0 to 1535, as said below
Outputs:
- features: bfloat16 [196608, 512], P(('scene', 'seg'))
The draws below stay inside these ranges and needn't reach their ends.
Inputs may be any that keep to these rules, and one draw needn't show every extreme that they name: zorder holds, for each device, a permutation of that device's 12 global block numbers. `image_row`: the row lies on a device of any scene group whose seg index equals that of the point's device. Within each scene group hilbert_target is a permutation of the group's block numbers; of one device's blocks at most 2 go to any one device, and in every draw some device hands exactly 2 blocks to another.
All inputs are finite; a program needn't handle non-finite values.
Results may differ from the reference program's by a relative error of at most 0.019.
Values may be sent and summed in bfloat16 or wider, within the bound.
A program may use at most 192 MiB of HBM per device.

```python
import jax
import jax.numpy as jnp
from jax import lax

C = 512
HID = 2048
IMGC = 1024
HEAD_DIM = 16
PATCH = 512
BLK = 128
LAYERS = 2
BLK_DEV = 12
IMG_DEV = 128
HEADS = 32
POINTS = 196608
BLOCKS = 1536
IMG_ROWS = 16384
N_SCENE = 8
N_SEG = 16
DEVICES = 128


def draw_zorder(key, part):
    keys = jax.random.split(jax.random.fold_in(key, 3), DEVICES)
    perms = jax.vmap(lambda single: jax.random.permutation(single, BLK_DEV))(keys)
    base = jnp.arange(DEVICES, dtype=jnp.int32)[:, None] * BLK_DEV
    return (perms.astype(jnp.int32) + base).reshape(-1)


def draw_image_row(key, part):
    first, second = jax.random.split(jax.random.fold_in(key, 11))
    device = jnp.arange(POINTS, dtype=jnp.int32) // (BLK_DEV * BLK)
    segment = device % N_SEG
    group = jax.random.randint(first, (POINTS,), 0, N_SCENE, dtype=jnp.int32)
    offset = jax.random.randint(second, (POINTS,), 0, IMG_DEV, dtype=jnp.int32)
    chosen = (group * N_SEG + segment) * IMG_DEV + offset
    return chosen.at[0].set(0).at[POINTS - 1].set(IMG_ROWS - 1)


def group_targets(key, group):
    keys = jax.random.split(key, 5)
    labels = jax.random.permutation(keys[0], N_SEG).astype(jnp.int32)
    lowest = (BLK_DEV + 1) // 2
    highest = min(BLK_DEV - 1, N_SEG) + 1
    single = jax.random.randint(keys[1], (), lowest, highest, dtype=jnp.int32)
    index = jnp.arange(BLK_DEV, dtype=jnp.int32)
    index = jnp.where(index < single, index, index - single)
    offsets = labels[index]
    shuffles = jax.vmap(lambda one: jax.random.permutation(one, BLK_DEV))(jax.random.split(keys[2], N_SEG))
    mapping = jax.random.permutation(keys[3], N_SEG).astype(jnp.int32)
    sources = jnp.arange(N_SEG, dtype=jnp.int32)[:, None]
    target_seg = mapping[(sources + offsets[shuffles]) % N_SEG].reshape(-1)
    tiebreak = jax.random.permutation(keys[4], N_SEG * BLK_DEV).astype(jnp.int32)
    order = jnp.argsort(target_seg * (N_SEG * BLK_DEV) + tiebreak)
    inverse = jnp.argsort(order).astype(jnp.int32)
    slot = inverse - target_seg * BLK_DEV
    return (group * N_SEG + target_seg) * BLK_DEV + slot


def draw_hilbert_target(key, part):
    keys = jax.random.split(jax.random.fold_in(key, 17), N_SCENE)
    groups = jnp.arange(N_SCENE, dtype=jnp.int32)
    return jax.vmap(group_targets)(keys, groups).reshape(-1).astype(jnp.int32)


def draw_in_weight(key, part):
    keys = jax.random.split(jax.random.fold_in(key, 7), 1)
    base = jax.random.normal(keys[0], (LAYERS, C, 3 * C), jnp.float32) * C ** (-0.5)
    return jnp.clip(base, -16.0, 16.0).astype(jnp.bfloat16)


def block_levels(stream_key, dims, pieces, low, high):
    level = 1.0
    for axis_at, shards_of in pieces:
        draws = jax.random.uniform(jax.random.fold_in(jax.random.fold_in(stream_key, 6), axis_at), (shards_of,), jnp.float32, low / len(pieces), high / len(pieces))
        level = level * jnp.repeat(jnp.exp(draws), dims[axis_at] // shards_of).reshape((-1,) + (1,) * (len(dims) - 1 - axis_at))
    return level


def bell_draw(key, extent, scale, bound, pieces=(), held_as=jnp.bfloat16):
    drawn = scale * jax.random.normal(key, extent, jnp.float32)
    if pieces:
        drawn = drawn * block_levels(key, extent, pieces, -0.22, 0.18)
    return jnp.clip(drawn, -bound, bound).astype(held_as)


def setup_inputs(seed: int = 0) -> dict:
    splits = jax.random.split(jax.random.key(seed), 12)
    points = bell_draw(splits[0], (POINTS, C), 1.0, 6.0, ((0, 128),))
    zorder = draw_zorder(jax.random.fold_in(splits[11], 71), 0)
    image = bell_draw(splits[2], (IMG_ROWS, IMGC), 1.0, 6.0, ((0, 128),))
    image_row = draw_image_row(jax.random.fold_in(splits[11], 71), 0)
    image_weight = bell_draw(splits[4], (IMGC, C), IMGC ** -0.5, 0.1875)
    norm_gain = jnp.clip(1.0 + 0.18 * jax.random.normal(splits[5], (LAYERS, 2, C), jnp.float32), 0.1, 1.9)
    in_weight = draw_in_weight(jax.random.fold_in(splits[11], 71), 0)
    out_weight = bell_draw(splits[7], (LAYERS, C, C), C ** -0.5, 0.25)
    up_weight = bell_draw(splits[8], (LAYERS, C, HID), C ** -0.5, 0.25)
    down_weight = bell_draw(splits[9], (LAYERS, HID, C), HID ** -0.5, 0.125)
    hilbert_target = draw_hilbert_target(jax.random.fold_in(splits[11], 71), 0)
    return {"points": points, "zorder": zorder, "image": image, "image_row": image_row, "image_weight": image_weight, "norm_gain": norm_gain, "in_weight": in_weight, "out_weight": out_weight, "up_weight": up_weight, "down_weight": down_weight, "hilbert_target": hilbert_target}


def normed(values, gain):
    center = values - lax.optimization_barrier(jnp.mean(values, axis=-1, keepdims=True))
    spread = lax.optimization_barrier(jnp.mean(center * center, axis=-1, keepdims=True))
    return (center * lax.rsqrt(spread + 1e-05) * gain).astype(jnp.bfloat16)

def attend(triple):
    query = triple[:, :C].reshape(PATCH, HEADS, HEAD_DIM).astype(jnp.float32)
    keys = triple[:, C:2 * C].reshape(PATCH, HEADS, HEAD_DIM).astype(jnp.float32)
    values = triple[:, 2 * C:].reshape(PATCH, HEADS, HEAD_DIM).astype(jnp.float32)
    scores = jnp.einsum('qhd,khd->hqk', query, keys) * HEAD_DIM ** (-0.5)
    scores = scores - lax.optimization_barrier(jnp.max(scores, axis=-1, keepdims=True))
    raised = jnp.exp(scores)
    weights = (raised / lax.optimization_barrier(jnp.sum(raised, axis=-1, keepdims=True))).astype(jnp.bfloat16)
    weights = lax.optimization_barrier(weights)
    mixed = jnp.einsum('hqk,khd->qhd', weights.astype(jnp.float32), values)
    return mixed.reshape(PATCH, C).astype(jnp.bfloat16)

def layer(features, gain, in_weight, out_weight, up_weight, down_weight):
    normal_one = normed(features, gain[0])
    triple = jnp.dot(normal_one, in_weight, preferred_element_type=jnp.float32).astype(jnp.bfloat16)
    mixed = attend(triple)
    after = features + jnp.dot(mixed, out_weight, preferred_element_type=jnp.float32)
    normal_two = normed(after, gain[1])
    hidden = jax.nn.gelu(jnp.dot(normal_two, up_weight, preferred_element_type=jnp.float32), approximate=False).astype(jnp.bfloat16)
    return after + jnp.dot(hidden, down_weight, preferred_element_type=jnp.float32)

def reference(points, zorder, image, image_row, image_weight, norm_gain, in_weight, out_weight, up_weight, down_weight, hilbert_target):
    image_proj = jnp.dot(image, image_weight, preferred_element_type=jnp.float32).astype(jnp.bfloat16)
    image_proj = lax.optimization_barrier(image_proj)
    joined = points.astype(jnp.float32) + jnp.take(image_proj, image_row, axis=0).astype(jnp.float32)
    zfeat = jnp.take(joined.reshape(BLOCKS, BLK, C), zorder, axis=0).reshape(-1, PATCH, C)

    def first_layer(patch):
        return layer(patch, norm_gain[0], in_weight[0], out_weight[0], up_weight[0], down_weight[0]).astype(jnp.bfloat16)

    def second_layer(patch):
        return layer(patch.astype(jnp.float32), norm_gain[1], in_weight[1], out_weight[1], up_weight[1], down_weight[1]).astype(jnp.bfloat16)
    first = lax.map(first_layer, zfeat)
    first = lax.optimization_barrier(first)
    hilbert = jnp.zeros((BLOCKS, BLK, C), jnp.bfloat16).at[hilbert_target].set(first.reshape(BLOCKS, BLK, C))
    second = lax.map(second_layer, hilbert.reshape(-1, PATCH, C))
    return second.reshape(POINTS, C)
```

```python
import functools

import jax
import jax.numpy as jnp
from jax import lax
from jax.experimental import pallas as pl
from jax.experimental.pallas import tpu as pltpu
from jax.sharding import PartitionSpec as P

HEAD_DIM = 16
PATCH = 512
EPS = 1e-05
LOG2E = 1.4426950408889634
MESH = pl.DeviceIdType.MESH
F32, BF16, I32 = jnp.float32, jnp.bfloat16, jnp.int32
NT = (((1,), (1,)), ((), ()))
ROWS, COLS = 16, 256
VMEM_LIMIT = 60 * 2**20


def mm(a, b):
    return jnp.dot(a, b, preferred_element_type=F32)


def image_kernel(n_scene, n_seg, blocks, image_ref, weight_ref, target_ref, table_ref, inverse_ref,
                 rows, columns, send, recv, fsend, frecv, tsend, trecv):
    scene = lax.axis_index("scene")
    seg = lax.axis_index("seg")
    core = scene % 2
    level = scene // 2
    chips = n_scene // 2
    other = level * 2 + 1 - core
    barrier = pltpu.get_barrier_semaphore()
    for k in range(1, chips):
        peer = (level + k) % chips * 2 + core
        pl.semaphore_signal(barrier, inc=1, device_id=(peer, seg), device_id_type=MESH)
    pl.semaphore_signal(barrier, inc=1, device_id=(other, seg), device_id_type=MESH)
    for k in range(1, n_seg):
        pl.semaphore_signal(barrier, inc=1, device_id=(scene, (seg + k) % n_seg), device_id_type=MESH)
    rows[scene] = mm(image_ref[...], weight_ref[...]).astype(BF16)
    columns[seg] = target_ref[...]
    pl.semaphore_wait(barrier, chips - 1 + 1 + n_seg - 1)

    def across(k):
        return pltpu.make_async_remote_copy(
            rows.at[scene], rows.at[scene], send.at[k], recv.at[k],
            device_id=((level + k) % chips * 2 + core, seg), device_id_type=MESH)

    def forward(k):
        held = (level + chips - k) % chips * 2 + core
        return pltpu.make_async_remote_copy(
            rows.at[held], rows.at[held], fsend.at[k], frecv.at[k],
            device_id=(other, seg), device_id_type=MESH)

    def targets(k):
        return pltpu.make_async_remote_copy(
            columns.at[seg], columns.at[seg], tsend.at[k], trecv.at[k],
            device_id=(scene, (seg + k) % n_seg), device_id_type=MESH)

    for k in (1, chips - 1, 2):
        across(k).start()
    forward(0).start()
    for k in range(1, n_seg):
        targets(k).start()
    for k in (1, chips - 1, 2):
        across(k).wait_recv()
        forward(k).start()
    for k in range(1, n_seg):
        targets(k).wait()
    base = scene * (n_seg * blocks)
    place = lax.broadcasted_iota(I32, (16, 128), 0)
    lane = lax.broadcasted_iota(I32, (16, 128), 1)
    within = place // 4 * (n_seg * 4) + place % 4
    for part in range(2):
        total = jnp.zeros((16, 128), I32)
        for source in range(n_seg):
            hit = columns[source] == lane + (base + part * 128)
            total = total + jnp.where(hit, within + source * 4, 0)
        summed = total[:8] + total[8:]
        for step in (4, 2, 1):
            summed = summed[:step] + summed[step:]
        inverse_ref[part:part + 1, :] = summed
    for k in range(chips):
        forward(k).wait_recv()
    for k in (1, chips - 1, 2):
        across(k).wait_send()
    for k in range(chips):
        forward(k).wait_send()
    table_ref[...] = rows[...].reshape(table_ref.shape)


def image_stage(image, weight, target, n_scene, n_seg):
    count, depth = image.shape
    width = weight.shape[1]
    blocks = target.shape[0]
    column = jnp.broadcast_to(jnp.pad(target, (0, 16 - blocks), constant_values=-1)[:, None], (16, 128))
    return pl.pallas_call(
        functools.partial(image_kernel, n_scene, n_seg, blocks),
        out_shape=(jax.ShapeDtypeStruct((n_scene * count, width), BF16), jax.ShapeDtypeStruct((2, 128), I32)),
        in_specs=[pl.BlockSpec(memory_space=pltpu.VMEM)] * 3,
        out_specs=(pl.BlockSpec(memory_space=pltpu.VMEM),) * 2,
        scratch_shapes=[
            pltpu.VMEM((n_scene, count, width), BF16),
            pltpu.VMEM((n_seg, 16, 128), I32),
            pltpu.SemaphoreType.DMA((n_scene // 2,)),
            pltpu.SemaphoreType.DMA((n_scene // 2,)),
            pltpu.SemaphoreType.DMA((n_scene // 2,)),
            pltpu.SemaphoreType.DMA((n_scene // 2,)),
            pltpu.SemaphoreType.DMA((n_seg,)),
            pltpu.SemaphoreType.DMA((n_seg,)),
        ],
        compiler_params=pltpu.CompilerParams(
            collective_id=0, has_side_effects=True, vmem_limit_bytes=VMEM_LIMIT),
    )(image, weight, column)


def normed(values, gain):
    center = values - jnp.mean(values, axis=-1, keepdims=True)
    spread = jnp.mean(center * center, axis=-1, keepdims=True)
    return (center * lax.rsqrt(spread + EPS) * gain).astype(BF16)


def gelu(values):
    return (0.5 * values * (1.0 + lax.erf(values * (0.5**0.5)))).astype(BF16)


def layer_patch(x, gain, w_in, w_out, w_up, w_down, query, key, value_t, mixed_t):
    width = x.shape[1]
    heads = width // HEAD_DIM
    normal = normed(x[...], gain[0:1, :])
    query[...] = (mm(normal, w_in[:, :width]) * (HEAD_DIM**-0.5 * LOG2E)).astype(BF16)
    key[...] = mm(normal, w_in[:, width:2 * width]).astype(BF16)
    value_t[...] = mm(normal, w_in[:, 2 * width:]).astype(BF16).T
    lane = lax.broadcasted_iota(I32, (PATCH, 128), 1) // HEAD_DIM

    def scores(i):
        group, head = i // 8, i % 8
        q = query[:, group * 128:(group + 1) * 128]
        q = jnp.where(lane == head, q, jnp.zeros((), BF16))
        k = key[:, group * 128:(group + 1) * 128]
        return lax.dot_general(q, k, NT, preferred_element_type=F32)

    def rest(i, score):
        raised = jnp.exp2(score - jnp.max(score, axis=1, keepdims=True)).astype(BF16)
        at = i * HEAD_DIM
        v = jnp.concatenate([value_t[at:at + HEAD_DIM, :], jnp.ones((16, PATCH), BF16)], axis=0)
        o = lax.dot_general(v, raised, NT, preferred_element_type=F32)
        mixed_t[at:at + HEAD_DIM, :] = (o[:HEAD_DIM] / o[HEAD_DIM:HEAD_DIM + 1]).astype(BF16)

    score = scores(0)
    for i in range(heads):
        following = scores(i + 1) if i + 1 < heads else None
        rest(i, score)
        score = following
    after = x[...] + mm(mixed_t[...].T, w_out[...])
    normal = normed(after, gain[1:2, :])
    hidden = w_up.shape[1]
    chunk = 512
    total = after
    up = mm(normal, w_up[:, :chunk])
    for at in range(0, hidden, chunk):
        following = mm(normal, w_up[:, at + chunk:at + 2 * chunk]) if at + chunk < hidden else None
        total = total + mm(gelu(up), w_down[at:at + chunk, :])
        up = following
    return total


def layers_kernel(n_seg, image_count, order_ref, inverse_ref, points_ref, image_row_ref, table_ref, gain_ref,
                  in_hbm, out_hbm, up_hbm, down_hbm, result_ref,
                  w_in, w_out, w_up, w_down, x, query, key, value_t, mixed_t,
                  send1, recv1, send2, recv2, wsem, ssem1, rsem1, ssem2, rsem2):
    scene = lax.axis_index("scene")
    me = lax.axis_index("seg")
    blocks = points_ref.shape[0]
    size = points_ref.shape[1]
    width = points_ref.shape[2]
    per = PATCH // size
    patches = blocks // per
    barrier = pltpu.get_barrier_semaphore()
    for k in range(1, n_seg):
        pl.semaphore_signal(barrier, inc=1, device_id=(scene, (me + k) % n_seg), device_id_type=MESH)
    loads = [
        [pltpu.make_async_copy(src.at[layer], dst.at[layer], wsem.at[layer, j])
         for j, (src, dst) in enumerate(((in_hbm, w_in), (out_hbm, w_out), (up_hbm, w_up), (down_hbm, w_down)))]
        for layer in range(2)
    ]
    for layer in range(2):
        for load in loads[layer]:
            load.start()
    for load in loads[0]:
        load.wait()
    pl.semaphore_wait(barrier, n_seg - 1)

    def piece(ref, patch, device):
        return ref.at[pl.ds((patch * n_seg + device) * per, per)]

    def copy1(patch, k):
        to = (me + k) % n_seg
        return pltpu.make_async_remote_copy(
            piece(send1, patch, to), piece(recv1, patch, me), ssem1.at[patch, k], rsem1.at[patch, k],
            device_id=(scene, to), device_id_type=MESH)

    def copy2(patch, k):
        to = (me + k) % n_seg
        return pltpu.make_async_remote_copy(
            piece(send2, patch, to), piece(recv2, patch, me), ssem2.at[patch, k], rsem2.at[patch, k],
            device_id=(scene, to), device_id_type=MESH)

    ORDER = [1, 4, 3, 12, 5, 15, 13, 7, 2, 8, 6, 9, 11, 14, 10]

    def compute(layer):
        return layer_patch(x, gain_ref.at[layer], w_in.at[layer], w_out.at[layer], w_up.at[layer],
                           w_down.at[layer], query, key, value_t, mixed_t)

    columns = width // COLS

    def first_patch(patch, carry):
        for b in range(per):
            block = lax.rem(order_ref[patch * per + b], blocks)
            row = image_row_ref[block]
            entry = lax.shift_right_logical(row, 11) * image_count + (row & (image_count - 1))
            count = table_ref.shape[0]
            hot = lax.broadcasted_iota(I32, (size, count), 1) == entry
            looked = mm(jnp.where(hot, 1.0, 0.0).astype(BF16), table_ref[...])
            x[b * size:(b + 1) * size, :] = points_ref[block].astype(F32) + looked
        out = compute(0).astype(BF16)
        for b in range(per):
            for r in range(size // ROWS):
                for c in range(columns):
                    send1[(patch * n_seg + r * columns + c) * per + b] = (
                        out[b * size + r * ROWS:b * size + (r + 1) * ROWS, c * COLS:(c + 1) * COLS])
        for k in ORDER:
            copy1(patch, k).start()
        for b in range(per):
            recv1[(patch * n_seg + me) * per + b] = send1[(patch * n_seg + me) * per + b]
        return carry

    lax.fori_loop(0, patches, first_patch, 0)
    for patch in range(patches):
        for k in ORDER:
            copy1(patch, k).wait_recv()
    for patch in range(patches):
        def fill(device, carry):
            for s in range(per):
                t = device * blocks + patch * per + s
                send2[(patch * n_seg + device) * per + s] = recv1[inverse_ref[t // 128, t % 128]]
            return carry

        lax.fori_loop(0, n_seg, fill, 0)
        for k in ORDER:
            copy2(patch, k).start()
        for s in range(per):
            recv2[(patch * n_seg + me) * per + s] = send2[(patch * n_seg + me) * per + s]
    for load in loads[1]:
        load.wait()

    def second_patch(patch, carry):
        for k in ORDER:
            copy2(patch, k).wait_recv()
        for s in range(per):
            for r in range(size // ROWS):
                for c in range(columns):
                    x[s * size + r * ROWS:s * size + (r + 1) * ROWS, c * COLS:(c + 1) * COLS] = (
                        recv2[(patch * n_seg + r * columns + c) * per + s].astype(F32))
        result_ref[pl.ds(patch * PATCH, PATCH), :] = compute(1).astype(BF16)
        return carry

    lax.fori_loop(0, patches, second_patch, 0)
    for patch in range(patches):
        for k in ORDER:
            copy1(patch, k).wait_send()
            copy2(patch, k).wait_send()


def layers_stage(n_seg, image_count, order, inverse, points, image_row, table, gain, w_in, w_out, w_up, w_down):
    length, width = points.shape
    blocks = order.shape[0]
    size = length // blocks
    patches = length // PATCH
    whole = pl.BlockSpec(memory_space=pltpu.VMEM)
    scalar = pl.BlockSpec(memory_space=pltpu.SMEM)
    hbm = pl.BlockSpec(memory_space=pl.ANY)
    pieces = (length // ROWS * (width // COLS), ROWS, COLS)
    dma = pltpu.SemaphoreType.DMA
    return pl.pallas_call(
        functools.partial(layers_kernel, n_seg, image_count),
        out_shape=jax.ShapeDtypeStruct((length, width), BF16),
        in_specs=[scalar, scalar, whole, whole, whole, whole, hbm, hbm, hbm, hbm],
        out_specs=whole,
        scratch_shapes=[
            pltpu.VMEM(w_in.shape, BF16),
            pltpu.VMEM(w_out.shape, BF16),
            pltpu.VMEM(w_up.shape, BF16),
            pltpu.VMEM(w_down.shape, BF16),
            pltpu.VMEM((PATCH, width), F32),
            pltpu.VMEM((PATCH, width), BF16),
            pltpu.VMEM((PATCH, width), BF16),
            pltpu.VMEM((width, PATCH), BF16),
            pltpu.VMEM((width, PATCH), BF16),
            pltpu.VMEM(pieces, BF16),
            pltpu.VMEM(pieces, BF16),
            pltpu.VMEM(pieces, BF16),
            pltpu.VMEM(pieces, BF16),
            dma((2, 4)),
            dma((patches, n_seg)),
            dma((patches, n_seg)),
            dma((patches, n_seg)),
            dma((patches, n_seg)),
        ],
        compiler_params=pltpu.CompilerParams(
            collective_id=1, has_side_effects=True, vmem_limit_bytes=VMEM_LIMIT),
    )(order, inverse, points.reshape(blocks, size, width), image_row.reshape(blocks, size, 1), table, gain,
      w_in, w_out, w_up, w_down)


def local(n_scene, n_seg, points, zorder, image, image_row, image_weight, norm_gain, in_weight, out_weight,
          up_weight, down_weight, hilbert_target):
    table, inverse = image_stage(image, image_weight, hilbert_target, n_scene, n_seg)
    return layers_stage(n_seg, image.shape[0], zorder, inverse, points, image_row, table, norm_gain,
                        in_weight, out_weight, up_weight, down_weight)


def solution(mesh):
    placed = (
        P(("scene", "seg"), None),
        P(("scene", "seg")),
        P(("scene", "seg"), None),
        P(("scene", "seg")),
        P(),
        P(),
        P(),
        P(),
        P(),
        P(),
        P(("scene", "seg")),
    )
    return jax.shard_map(
        functools.partial(local, mesh.shape["scene"], mesh.shape["seg"]),
        mesh=mesh, in_specs=placed, out_specs=P(("scene", "seg"), None), check_vma=False)
```

```python
import functools

import jax
import jax.numpy as jnp
from jax import lax
from jax.experimental import pallas as pl
from jax.experimental.pallas import tpu as pltpu
from jax.sharding import PartitionSpec as P

HEAD_DIM = 16
PATCH = 512
EPS = 1e-05
LOG2E = 1.4426950408889634
MESH = pl.DeviceIdType.MESH
F32, BF16, I32 = jnp.float32, jnp.bfloat16, jnp.int32
NT = (((1,), (1,)), ((), ()))
ROWS, COLS = 16, 256
VMEM_LIMIT = 60 * 2**20


def mm(a, b):
    return jnp.dot(a, b, preferred_element_type=F32)


def normed(values, gain):
    center = values - jnp.mean(values, axis=-1, keepdims=True)
    spread = jnp.mean(center * center, axis=-1, keepdims=True)
    return (center * lax.rsqrt(spread + EPS) * gain).astype(BF16)


def gelu(values):
    return (0.5 * values * (1.0 + lax.erf(values * (0.5**0.5)))).astype(BF16)


def layer_patch(x, gain, w_in, w_out, w_up, w_down, query, key, value_t, mixed_t):
    width = x.shape[1]
    heads = width // HEAD_DIM
    normal = normed(x[...], gain[0:1, :])
    query[...] = (mm(normal, w_in[:, :width]) * (HEAD_DIM**-0.5 * LOG2E)).astype(BF16)
    key[...] = mm(normal, w_in[:, width:2 * width]).astype(BF16)
    value_t[...] = mm(normal, w_in[:, 2 * width:]).astype(BF16).T
    lane = lax.broadcasted_iota(I32, (PATCH, 128), 1) // HEAD_DIM

    def scores(i):
        group, head = i // 8, i % 8
        q = query[:, group * 128:(group + 1) * 128]
        q = jnp.where(lane == head, q, jnp.zeros((), BF16))
        k = key[:, group * 128:(group + 1) * 128]
        return lax.dot_general(q, k, NT, preferred_element_type=F32)

    def raised(score):
        return jnp.exp2(score - jnp.max(score, axis=1, keepdims=True)).astype(BF16)

    def mix(i, weights):
        at = i * HEAD_DIM
        v = jnp.concatenate([value_t[at:at + HEAD_DIM, :], jnp.ones((16, PATCH), BF16)], axis=0)
        o = lax.dot_general(v, weights, NT, preferred_element_type=F32)
        mixed_t[at:at + HEAD_DIM, :] = (o[:HEAD_DIM] / o[HEAD_DIM:HEAD_DIM + 1]).astype(BF16)

    score, weights = scores(0), None
    for i in range(heads):
        following = scores(i + 1) if i + 1 < heads else None
        exponents = raised(score)
        if i > 0:
            mix(i - 1, weights)
        score, weights = following, exponents
    mix(heads - 1, weights)
    after = x[...] + mm(mixed_t[...].T, w_out[...])
    normal = normed(after, gain[1:2, :])
    hidden = w_up.shape[1]
    chunk = 512
    total = after
    up = mm(normal, w_up[:, :chunk])
    for at in range(0, hidden, chunk):
        following = mm(normal, w_up[:, at + chunk:at + 2 * chunk]) if at + chunk < hidden else None
        total = total + mm(gelu(up), w_down[at:at + chunk, :])
        up = following
    return total


ORDER = (1, 4, 3, 12, 5, 15, 13, 7, 2, 8, 6, 9, 11, 14, 10)


def kernel(n_scene, n_seg, order_ref, target_ref, gain_ref, image_row_ref,
           image_hbm, weight_hbm, points_hbm, in_hbm, out_hbm, up_hbm, down_hbm, result_ref,
           image, image_weight, points, w_in, w_out, w_up, w_down,
           table, targets, inverse_v, inverse, x, query, key, value_t, mixed_t,
           send1, recv1, send2, recv2,
           wsem, psem, isem, asend, arecv, fsend, frecv, tsend, trecv, ssem1, rsem1, ssem2, rsem2):
    scene = lax.axis_index("scene")
    me = lax.axis_index("seg")
    blocks, size, width = points.shape
    per = PATCH // size
    patches = blocks // per
    columns = width // COLS
    count = image.shape[0]
    side = 4
    core = scene % 2
    level = scene // 2
    chips = n_scene // 2
    other = level * 2 + 1 - core

    def peer(k):
        return (me // side + k // side) % side * side + (me + k) % side

    barrier = pltpu.get_barrier_semaphore()
    for k in range(1, chips):
        pl.semaphore_signal(barrier, inc=1, device_id=((level + k) % chips * 2 + core, me), device_id_type=MESH)
    pl.semaphore_signal(barrier, inc=1, device_id=(other, me), device_id_type=MESH)
    for k in range(1, n_seg):
        pl.semaphore_signal(barrier, inc=1, device_id=(scene, peer(k)), device_id_type=MESH)

    first = [pltpu.make_async_copy(image_hbm, image, isem.at[0]),
             pltpu.make_async_copy(weight_hbm, image_weight, isem.at[1])]
    load_points = pltpu.make_async_copy(points_hbm, points, psem.at[0])
    loads = [
        [pltpu.make_async_copy(src.at[layer], dst.at[layer], wsem.at[layer, j])
         for j, (src, dst) in enumerate(((in_hbm, w_in), (out_hbm, w_out), (up_hbm, w_up), (down_hbm, w_down)))]
        for layer in range(2)
    ]
    for load in first + [load_points] + loads[0] + loads[1]:
        load.start()

    sublane = lax.broadcasted_iota(I32, (16, 128), 0)
    column = jnp.full((16, 128), -1, I32)
    for j in range(blocks):
        column = jnp.where(sublane == j, target_ref[j], column)
    targets[me] = column
    for load in first:
        load.wait()
    table[scene] = mm(image[...], image_weight[...]).astype(BF16)
    pl.semaphore_wait(barrier, chips + n_seg - 1)

    def across(k):
        return pltpu.make_async_remote_copy(
            table.at[scene], table.at[scene], asend.at[k], arecv.at[k],
            device_id=((level + k) % chips * 2 + core, me), device_id_type=MESH)

    def forward(k):
        held = (level + chips - k) % chips * 2 + core
        return pltpu.make_async_remote_copy(
            table.at[held], table.at[held], fsend.at[k], frecv.at[k],
            device_id=(other, me), device_id_type=MESH)

    def tell(k):
        return pltpu.make_async_remote_copy(
            targets.at[me], targets.at[me], tsend.at[k], trecv.at[k],
            device_id=(scene, peer(k)), device_id_type=MESH)

    hops = [k for k in (1, chips - 1, 2)]
    for k in hops:
        across(k).start()
    forward(0).start()
    for k in ORDER:
        tell(k).start()
    for k in hops[:2]:
        across(k).wait_recv()
        forward(k).start()
    for k in ORDER:
        tell(k).wait_recv()
    base = scene * (n_seg * blocks)
    lane = lax.broadcasted_iota(I32, (16, 128), 1)
    within = sublane // per * (n_seg * per) + sublane % per
    for part in range(2):
        total = jnp.zeros((16, 128), I32)
        for source in range(n_seg):
            hit = targets[source] == lane + (base + part * 128)
            total = total + jnp.where(hit, within + source * per, 0)
        summed = total[:8] + total[8:]
        for step in (4, 2, 1):
            summed = summed[:step] + summed[step:]
        summed = jnp.minimum(summed, n_seg * blocks - 1)
        inverse_v[part * 8:(part + 1) * 8, :] = jnp.broadcast_to(summed, (8, 128))
    to_scalars = pltpu.make_async_copy(inverse_v, inverse, isem.at[2])
    to_scalars.start()
    across(2).wait_recv()
    forward(2).start()
    row = image_row_ref[...]
    entry = lax.shift_right_logical(row, 11) * count + (row & (count - 1))
    entry = jnp.concatenate([entry, jnp.zeros((16 - blocks, size), I32)], axis=0).astype(F32).T
    pick = lax.broadcasted_iota(I32, (size, 16), 1)
    rows = lax.broadcasted_iota(I32, (size, n_scene * count), 1)
    load_points.wait()
    for load in loads[0]:
        load.wait()
    for k in range(chips):
        forward(k).wait_recv()
    to_scalars.wait()

    def piece(ref, patch, device):
        return ref.at[pl.ds((patch * n_seg + device) * per, per)]

    def copy1(patch, k):
        return pltpu.make_async_remote_copy(
            piece(send1, patch, peer(k)), piece(recv1, patch, me), ssem1.at[patch, k], rsem1.at[patch, k],
            device_id=(scene, peer(k)), device_id_type=MESH)

    def copy2(patch, k):
        return pltpu.make_async_remote_copy(
            piece(send2, patch, peer(k)), piece(recv2, patch, me), ssem2.at[patch, k], rsem2.at[patch, k],
            device_id=(scene, peer(k)), device_id_type=MESH)

    def compute(layer):
        return layer_patch(x, gain_ref.at[layer], w_in.at[layer], w_out.at[layer], w_up.at[layer],
                           w_down.at[layer], query, key, value_t, mixed_t)

    def first_patch(patch, carry):
        for b in range(per):
            block = lax.rem(order_ref[patch * per + b], blocks)
            mine = jnp.sum(jnp.where(pick == block, entry, 0.0), axis=1, keepdims=True).astype(I32)
            hot = jnp.where(rows == mine, 1.0, 0.0).astype(BF16)
            looked = mm(hot, table[...].reshape(n_scene * count, width))
            x[b * size:(b + 1) * size, :] = points[block].astype(F32) + looked
        out = compute(0).astype(BF16)
        for b in range(per):
            for r in range(size // ROWS):
                for c in range(columns):
                    send1[(patch * n_seg + r * columns + c) * per + b] = (
                        out[b * size + r * ROWS:b * size + (r + 1) * ROWS, c * COLS:(c + 1) * COLS])
        for k in ORDER:
            copy1(patch, k).start()
        for b in range(per):
            recv1[(patch * n_seg + me) * per + b] = send1[(patch * n_seg + me) * per + b]
        return carry

    lax.fori_loop(0, patches, first_patch, 0)
    for patch in range(patches):
        for k in ORDER:
            copy1(patch, k).wait_recv()

    def send_patch(patch):
        for k in ORDER:
            copy2(patch, k).start()

    for patch in range(patches):
        def fill(device, carry):
            for s in range(per):
                t = device * blocks + patch * per + s
                send2[(patch * n_seg + device) * per + s] = recv1[inverse[t // 128 * 8, t % 128]]
            return carry

        lax.fori_loop(0, n_seg, fill, 0)
        if patch == 0:
            send_patch(0)
        for s in range(per):
            recv2[(patch * n_seg + me) * per + s] = send2[(patch * n_seg + me) * per + s]
    for load in loads[1]:
        load.wait()

    def second_patch(patch, carry):
        for k in ORDER:
            copy2(patch, k).wait_recv()

        @pl.when(patch + 1 < patches)
        def _():
            send_patch(patch + 1)

        for s in range(per):
            for r in range(size // ROWS):
                for c in range(columns):
                    x[s * size + r * ROWS:s * size + (r + 1) * ROWS, c * COLS:(c + 1) * COLS] = (
                        recv2[(patch * n_seg + r * columns + c) * per + s].astype(F32))
        result_ref[pl.ds(patch * PATCH, PATCH), :] = compute(1).astype(BF16)
        return carry

    lax.fori_loop(0, patches, second_patch, 0)
    for k in hops:
        across(k).wait_send()
    for k in range(chips):
        forward(k).wait_send()
    for k in ORDER:
        tell(k).wait_send()
    for patch in range(patches):
        for k in ORDER:
            copy1(patch, k).wait_send()
            copy2(patch, k).wait_send()


def local(n_scene, n_seg, points, zorder, image, image_row, image_weight, norm_gain, in_weight, out_weight,
          up_weight, down_weight, hilbert_target):
    length, width = points.shape
    blocks = zorder.shape[0]
    size = length // blocks
    patches = length // PATCH
    count = image.shape[0]
    chips = n_scene // 2
    whole = pl.BlockSpec(memory_space=pltpu.VMEM)
    scalar = pl.BlockSpec(memory_space=pltpu.SMEM)
    hbm = pl.BlockSpec(memory_space=pl.ANY)
    pieces = (length // ROWS * (width // COLS), ROWS, COLS)
    dma = pltpu.SemaphoreType.DMA
    return pl.pallas_call(
        functools.partial(kernel, n_scene, n_seg),
        out_shape=jax.ShapeDtypeStruct((length, width), BF16),
        in_specs=[scalar, scalar, whole, whole] + [hbm] * 7,
        out_specs=whole,
        scratch_shapes=[
            pltpu.VMEM(image.shape, BF16),
            pltpu.VMEM(image_weight.shape, BF16),
            pltpu.VMEM((blocks, size, width), BF16),
            pltpu.VMEM(in_weight.shape, BF16),
            pltpu.VMEM(out_weight.shape, BF16),
            pltpu.VMEM(up_weight.shape, BF16),
            pltpu.VMEM(down_weight.shape, BF16),
            pltpu.VMEM((n_scene, count, width), BF16),
            pltpu.VMEM((n_seg, 16, 128), I32),
            pltpu.VMEM((16, 128), I32),
            pltpu.SMEM((16, 128), I32),
            pltpu.VMEM((PATCH, width), F32),
            pltpu.VMEM((PATCH, width), BF16),
            pltpu.VMEM((PATCH, width), BF16),
            pltpu.VMEM((width, PATCH), BF16),
            pltpu.VMEM((width, PATCH), BF16),
            pltpu.VMEM(pieces, BF16),
            pltpu.VMEM(pieces, BF16),
            pltpu.VMEM(pieces, BF16),
            pltpu.VMEM(pieces, BF16),
            dma((2, 4)),
            dma((1,)),
            dma((3,)),
            dma((chips,)),
            dma((chips,)),
            dma((chips,)),
            dma((chips,)),
            dma((n_seg,)),
            dma((n_seg,)),
            dma((patches, n_seg)),
            dma((patches, n_seg)),
            dma((patches, n_seg)),
            dma((patches, n_seg)),
        ],
        compiler_params=pltpu.CompilerParams(
            collective_id=0, has_side_effects=True, vmem_limit_bytes=VMEM_LIMIT),
    )(zorder, hilbert_target, norm_gain, image_row.reshape(blocks, size), image, image_weight,
      points.reshape(blocks, size, width), in_weight, out_weight, up_weight, down_weight)


def solution(mesh):
    placed = (
        P(("scene", "seg"), None),
        P(("scene", "seg")),
        P(("scene", "seg"), None),
        P(("scene", "seg")),
        P(),
        P(),
        P(),
        P(),
        P(),
        P(),
        P(("scene", "seg")),
    )
    return jax.shard_map(
        functools.partial(local, mesh.shape["scene"], mesh.shape["seg"]),
        mesh=mesh, in_specs=placed, out_specs=P(("scene", "seg"), None), check_vma=False)
```

```python
import functools

import jax
import jax.numpy as jnp
from jax import lax
from jax.experimental import pallas as pl
from jax.experimental.pallas import tpu as pltpu
from jax.sharding import PartitionSpec as P

HEAD_DIM = 16
PATCH = 512
EPS = 1e-05
LOG2E = 1.4426950408889634
MESH = pl.DeviceIdType.MESH
F32, BF16, I32 = jnp.float32, jnp.bfloat16, jnp.int32
NT = (((1,), (1,)), ((), ()))
ROWS, COLS = 16, 256
VMEM_LIMIT = 61 * 2**20


def mm(a, b):
    return jnp.dot(a, b, preferred_element_type=F32)


def normed(values, gain):
    center = values - jnp.mean(values, axis=-1, keepdims=True)
    spread = jnp.mean(center * center, axis=-1, keepdims=True)
    return (center * lax.rsqrt(spread + EPS) * gain).astype(BF16)


def gelu(values):
    return (0.5 * values * (1.0 + lax.erf(values * (0.5**0.5)))).astype(BF16)


def layer_patch(x, gain, w_in, w_out, w_up, w_down, query, key, value_t, mixed_t, parts, emit):
    width = x.shape[1]
    heads = width // HEAD_DIM
    normal = normed(x[...], gain[0:1, :])
    query[...] = (mm(normal, w_in[:, :width]) * (HEAD_DIM**-0.5 * LOG2E)).astype(BF16)
    key[...] = mm(normal, w_in[:, width:2 * width]).astype(BF16)
    value_t[...] = mm(normal, w_in[:, 2 * width:]).astype(BF16).T
    half = 256
    lane = lax.broadcasted_iota(I32, (half, 128), 1) // HEAD_DIM

    def scores(step):
        part, i = step
        group, head = i // 8, i % 8
        q = query[part * half:(part + 1) * half, group * 128:(group + 1) * 128]
        q = jnp.where(lane == head, q, jnp.zeros((), BF16))
        k = key[:, group * 128:(group + 1) * 128]
        return lax.dot_general(q, k, NT, preferred_element_type=F32)

    def raised(score):
        return jnp.exp2(score - jnp.max(score, axis=1, keepdims=True)).astype(BF16)

    def mix(step, weights):
        part, i = step
        at = i * HEAD_DIM
        v = jnp.concatenate([value_t[at:at + HEAD_DIM, :], jnp.ones((16, PATCH), BF16)], axis=0)
        o = lax.dot_general(v, weights, NT, preferred_element_type=F32)
        mixed_t[at:at + HEAD_DIM, part * half:(part + 1) * half] = (
            o[:HEAD_DIM] / o[HEAD_DIM:HEAD_DIM + 1]).astype(BF16)

    def finish(part, rows):
        at = slice(part * rows, (part + 1) * rows)
        after = x[at, :] + mm(mixed_t[:, at].T, w_out[...])
        normal = normed(after, gain[1:2, :])
        hidden = w_up.shape[1]
        chunk = 512
        total = after
        up = mm(normal, w_up[:, :chunk])
        for at in range(0, hidden, chunk):
            following = mm(normal, w_up[:, at + chunk:at + 2 * chunk]) if at + chunk < hidden else None
            total = total + mm(gelu(up), w_down[at:at + chunk, :])
            up = following
        emit(part, total)

    steps = [(part, i) for part in range(PATCH // half) for i in range(heads)]
    lead, lag = 2, 2
    score = {n: scores(steps[n]) for n in range(lead)}
    weights = {}
    for n in range(len(steps) + lag):
        if n + lead < len(steps):
            score[n + lead] = scores(steps[n + lead])
        if n < len(steps):
            weights[n] = raised(score.pop(n))
        if n >= lag:
            mix(steps[n - lag], weights.pop(n - lag))
            if parts > 1 and n - lag + 1 == heads:
                finish(0, half)
    if parts > 1:
        finish(1, half)
    else:
        finish(0, PATCH)


ORDER = (1, 4, 3, 12, 5, 15, 13, 7, 2, 8, 6, 9, 11, 14, 10)


def kernel(n_scene, n_seg, order_ref, target_ref, gain_ref, image_row_ref,
           image_hbm, weight_hbm, points_hbm, in_hbm, out_hbm, up_hbm, down_hbm, result_ref,
           image, image_weight, points, w_in, w_out, w_up, w_down,
           table, targets, inverse_v, inverse, hot, x, query, key, value_t, mixed_t,
           send1, recv1, send2, recv2,
           wsem, psem, isem, asend, arecv, fsend, frecv, tsend, trecv, ssem1, rsem1, ssem2, rsem2):
    scene = lax.axis_index("scene")
    me = lax.axis_index("seg")
    blocks, size, width = points.shape
    per = PATCH // size
    patches = blocks // per
    columns = width // COLS
    count = image.shape[0]
    side = 4
    core = scene % 2
    level = scene // 2
    chips = n_scene // 2
    other = level * 2 + 1 - core

    def peer(k):
        return (me // side + k // side) % side * side + (me + k) % side

    barrier = pltpu.get_barrier_semaphore()
    for k in range(1, chips):
        pl.semaphore_signal(barrier, inc=1, device_id=((level + k) % chips * 2 + core, me), device_id_type=MESH)
    pl.semaphore_signal(barrier, inc=1, device_id=(other, me), device_id_type=MESH)
    for k in range(1, n_seg):
        pl.semaphore_signal(barrier, inc=1, device_id=(scene, peer(k)), device_id_type=MESH)

    first = [pltpu.make_async_copy(image_hbm, image, isem.at[0]),
             pltpu.make_async_copy(weight_hbm, image_weight, isem.at[1])]
    load_points = pltpu.make_async_copy(points_hbm, points, psem.at[0])
    loads = [
        [pltpu.make_async_copy(src.at[layer], dst.at[layer], wsem.at[layer, j])
         for j, (src, dst) in enumerate(((in_hbm, w_in), (out_hbm, w_out), (up_hbm, w_up), (down_hbm, w_down)))]
        for layer in range(2)
    ]
    for load in first + [load_points] + loads[0] + loads[1]:
        load.start()

    sublane = lax.broadcasted_iota(I32, (16, 128), 0)
    column = jnp.full((16, 128), -1, I32)
    for j in range(blocks):
        column = jnp.where(sublane == j, target_ref[j], column)
    targets[me] = column
    for load in first:
        load.wait()
    table[scene] = mm(image[...], image_weight[...]).astype(BF16)
    pl.semaphore_wait(barrier, chips + n_seg - 1)

    def across(k):
        return pltpu.make_async_remote_copy(
            table.at[scene], table.at[scene], asend.at[k], arecv.at[k],
            device_id=((level + k) % chips * 2 + core, me), device_id_type=MESH)

    def forward(k):
        held = (level + chips - k) % chips * 2 + core
        return pltpu.make_async_remote_copy(
            table.at[held], table.at[held], fsend.at[k], frecv.at[k],
            device_id=(other, me), device_id_type=MESH)

    def tell(k):
        return pltpu.make_async_remote_copy(
            targets.at[me], targets.at[me], tsend.at[k], trecv.at[k],
            device_id=(scene, peer(k)), device_id_type=MESH)

    hops = [k for k in (1, chips - 1, 2)]
    for k in hops:
        across(k).start()
    forward(0).start()
    for k in ORDER:
        tell(k).start()
    for k in hops[:2]:
        across(k).wait_recv()
        forward(k).start()
    for k in ORDER:
        tell(k).wait_recv()
    base = scene * (n_seg * blocks)
    lane = lax.broadcasted_iota(I32, (16, 128), 1)
    within = sublane // per * (n_seg * per) + sublane % per
    for part in range(2):
        total = jnp.zeros((16, 128), I32)
        for source in range(n_seg):
            hit = targets[source] == lane + (base + part * 128)
            total = total + jnp.where(hit, within + source * per, 0)
        summed = total[:8] + total[8:]
        for step in (4, 2, 1):
            summed = summed[:step] + summed[step:]
        summed = jnp.minimum(summed, n_seg * blocks - 1)
        inverse_v[part * 8:(part + 1) * 8, :] = jnp.broadcast_to(summed, (8, 128))
    to_scalars = pltpu.make_async_copy(inverse_v, inverse, isem.at[2])
    to_scalars.start()
    across(2).wait_recv()
    forward(2).start()
    row = image_row_ref[...]
    entry = lax.shift_right_logical(row, 11) * count + (row & (count - 1))
    entry = jnp.concatenate([entry, jnp.zeros((16 - blocks, size), I32)], axis=0).astype(F32).T
    pick = lax.broadcasted_iota(I32, (size, 16), 1)
    rows = lax.broadcasted_iota(I32, (size, n_scene * count), 1)
    for b in range(blocks):
        block = lax.rem(order_ref[b], blocks)
        mine = jnp.sum(jnp.where(pick == block, entry, 0.0), axis=1, keepdims=True).astype(I32)
        hot[b * size:(b + 1) * size, :] = jnp.where(rows == mine, 1.0, 0.0).astype(BF16)
    load_points.wait()
    for load in loads[0]:
        load.wait()
    for k in range(chips):
        forward(k).wait_recv()
    to_scalars.wait()

    def piece(ref, patch, device):
        return ref.at[pl.ds((patch * n_seg + device) * per, per)]

    def copy1(patch, part, k):
        ranks = per // 2
        there = pl.ds((patch * n_seg + peer(k)) * per + part * ranks, ranks)
        here = pl.ds((patch * n_seg + me) * per + part * ranks, ranks)
        return pltpu.make_async_remote_copy(
            send1.at[there], recv1.at[here], ssem1.at[patch * 2 + part, k], rsem1.at[patch * 2 + part, k],
            device_id=(scene, peer(k)), device_id_type=MESH)

    def copy2(patch, k):
        return pltpu.make_async_remote_copy(
            piece(send2, patch, peer(k)), piece(recv2, patch, me), ssem2.at[patch, k], rsem2.at[patch, k],
            device_id=(scene, peer(k)), device_id_type=MESH)

    def compute(layer, parts, emit):
        layer_patch(x, gain_ref.at[layer], w_in.at[layer], w_out.at[layer], w_up.at[layer],
                    w_down.at[layer], query, key, value_t, mixed_t, parts, emit)

    def first_patch(patch, carry):
        at = pl.ds(patch * PATCH, PATCH)
        x[...] = mm(hot[at, :], table[...].reshape(n_scene * count, width))
        for b in range(per):
            block = lax.rem(order_ref[patch * per + b], blocks)
            x[b * size:(b + 1) * size, :] += points[block].astype(F32)

        def emit(part, result):
            out = result.astype(BF16)
            for j in range(per // 2):
                b = part * (per // 2) + j
                for r in range(size // ROWS):
                    for c in range(columns):
                        send1[(patch * n_seg + r * columns + c) * per + b] = (
                            out[j * size + r * ROWS:j * size + (r + 1) * ROWS, c * COLS:(c + 1) * COLS])
            for k in ORDER:
                copy1(patch, part, k).start()

        compute(0, 2, emit)
        for b in range(per):
            recv1[(patch * n_seg + me) * per + b] = send1[(patch * n_seg + me) * per + b]
        return carry

    lax.fori_loop(0, patches, first_patch, 0)
    for patch in range(patches):
        for part in range(2):
            for k in ORDER:
                copy1(patch, part, k).wait_recv()

    def send_patch(patch):
        for k in ORDER:
            copy2(patch, k).start()

    for patch in range(patches):
        def fill(device, carry):
            for s in range(per):
                t = device * blocks + patch * per + s
                send2[(patch * n_seg + device) * per + s] = recv1[inverse[t // 128 * 8, t % 128]]
            return carry

        lax.fori_loop(0, n_seg, fill, 0)
        if patch == 0:
            send_patch(0)
        for s in range(per):
            recv2[(patch * n_seg + me) * per + s] = send2[(patch * n_seg + me) * per + s]
    for load in loads[1]:
        load.wait()

    def second_patch(patch, carry):
        for k in ORDER:
            copy2(patch, k).wait_recv()

        @pl.when(patch + 1 < patches)
        def _():
            send_patch(patch + 1)

        for s in range(per):
            for r in range(size // ROWS):
                for c in range(columns):
                    x[s * size + r * ROWS:s * size + (r + 1) * ROWS, c * COLS:(c + 1) * COLS] = (
                        recv2[(patch * n_seg + r * columns + c) * per + s].astype(F32))

        def emit(part, result):
            result_ref[pl.ds(patch * PATCH, PATCH), :] = result.astype(BF16)

        compute(1, 1, emit)
        return carry

    lax.fori_loop(0, patches, second_patch, 0)
    for k in hops:
        across(k).wait_send()
    for k in range(chips):
        forward(k).wait_send()
    for k in ORDER:
        tell(k).wait_send()
    for patch in range(patches):
        for k in ORDER:
            copy1(patch, 0, k).wait_send()
            copy1(patch, 1, k).wait_send()
            copy2(patch, k).wait_send()


def local(n_scene, n_seg, points, zorder, image, image_row, image_weight, norm_gain, in_weight, out_weight,
          up_weight, down_weight, hilbert_target):
    length, width = points.shape
    blocks = zorder.shape[0]
    size = length // blocks
    patches = length // PATCH
    count = image.shape[0]
    chips = n_scene // 2
    whole = pl.BlockSpec(memory_space=pltpu.VMEM)
    scalar = pl.BlockSpec(memory_space=pltpu.SMEM)
    hbm = pl.BlockSpec(memory_space=pl.ANY)
    pieces = (length // ROWS * (width // COLS), ROWS, COLS)
    dma = pltpu.SemaphoreType.DMA
    return pl.pallas_call(
        functools.partial(kernel, n_scene, n_seg),
        out_shape=pltpu.VMEM((length, width), BF16),
        in_specs=[scalar, scalar, whole, whole] + [hbm] * 7,
        out_specs=whole,
        scratch_shapes=[
            pltpu.VMEM(image.shape, BF16),
            pltpu.VMEM(image_weight.shape, BF16),
            pltpu.VMEM((blocks, size, width), BF16),
            pltpu.VMEM(in_weight.shape, BF16),
            pltpu.VMEM(out_weight.shape, BF16),
            pltpu.VMEM(up_weight.shape, BF16),
            pltpu.VMEM(down_weight.shape, BF16),
            pltpu.VMEM((n_scene, count, width), BF16),
            pltpu.VMEM((n_seg, 16, 128), I32),
            pltpu.VMEM((16, 128), I32),
            pltpu.SMEM((16, 128), I32),
            pltpu.VMEM((length, n_scene * count), BF16),
            pltpu.VMEM((PATCH, width), F32),
            pltpu.VMEM((PATCH, width), BF16),
            pltpu.VMEM((PATCH, width), BF16),
            pltpu.VMEM((width, PATCH), BF16),
            pltpu.VMEM((width, PATCH), BF16),
            pltpu.VMEM(pieces, BF16),
            pltpu.VMEM(pieces, BF16),
            pltpu.VMEM(pieces, BF16),
            pltpu.VMEM(pieces, BF16),
            dma((2, 4)),
            dma((1,)),
            dma((3,)),
            dma((chips,)),
            dma((chips,)),
            dma((chips,)),
            dma((chips,)),
            dma((n_seg,)),
            dma((n_seg,)),
            dma((patches * 2, n_seg)),
            dma((patches * 2, n_seg)),
            dma((patches, n_seg)),
            dma((patches, n_seg)),
        ],
        compiler_params=pltpu.CompilerParams(
            collective_id=0, has_side_effects=True, vmem_limit_bytes=VMEM_LIMIT),
    )(zorder, hilbert_target, norm_gain, image_row.reshape(blocks, size), image, image_weight,
      points.reshape(blocks, size, width), in_weight, out_weight, up_weight, down_weight)


def solution(mesh):
    placed = (
        P(("scene", "seg"), None),
        P(("scene", "seg")),
        P(("scene", "seg"), None),
        P(("scene", "seg")),
        P(),
        P(),
        P(),
        P(),
        P(),
        P(),
        P(("scene", "seg")),
    )
    return jax.shard_map(
        functools.partial(local, mesh.shape["scene"], mesh.shape["seg"]),
        mesh=mesh, in_specs=placed, out_specs=P(("scene", "seg"), None), check_vma=False)
```

```python
import functools

import jax
import jax.numpy as jnp
from jax import lax
from jax.experimental import pallas as pl
from jax.experimental.pallas import tpu as pltpu
from jax.sharding import PartitionSpec as P

HEAD_DIM = 16
PATCH = 512
EPS = 1e-05
LOG2E = 1.4426950408889634
MESH = pl.DeviceIdType.MESH
F32, BF16, I32 = jnp.float32, jnp.bfloat16, jnp.int32
NT = (((1,), (1,)), ((), ()))
ROWS, COLS = 16, 256
VMEM_LIMIT = 61 * 2**20


def mm(a, b):
    return jnp.dot(a, b, preferred_element_type=F32)


def normed(values, gain):
    center = values - jnp.mean(values, axis=-1, keepdims=True)
    spread = jnp.mean(center * center, axis=-1, keepdims=True)
    return (center * lax.rsqrt(spread + EPS) * gain).astype(BF16)


def gelu(values):
    return (0.5 * values * (1.0 + lax.erf(values * (0.5**0.5)))).astype(BF16)


def layer_patch(x, gain, w_in, w_out, w_up, w_down, query, key, value_t, mixed_t, parts, emit):
    width = x.shape[1]
    heads = width // HEAD_DIM
    normal = normed(x[...], gain[0:1, :])
    query[...] = (mm(normal, w_in[:, :width]) * (HEAD_DIM**-0.5 * LOG2E)).astype(BF16)
    key[...] = mm(normal, w_in[:, width:2 * width]).astype(BF16)
    value_t[...] = mm(normal, w_in[:, 2 * width:]).astype(BF16).T
    half = 256
    lane = lax.broadcasted_iota(I32, (half, 128), 1) // HEAD_DIM

    def scores(step):
        part, i = step
        group, head = i // 8, i % 8
        q = query[part * half:(part + 1) * half, group * 128:(group + 1) * 128]
        q = jnp.where(lane == head, q, jnp.zeros((), BF16))
        k = key[:, group * 128:(group + 1) * 128]
        return lax.dot_general(q, k, NT, preferred_element_type=F32)

    def raised(score):
        return jnp.exp2(score - jnp.max(score, axis=1, keepdims=True)).astype(BF16)

    def mix(step, weights):
        part, i = step
        at = i * HEAD_DIM
        v = jnp.concatenate([value_t[at:at + HEAD_DIM, :], jnp.ones((16, PATCH), BF16)], axis=0)
        o = lax.dot_general(v, weights, NT, preferred_element_type=F32)
        mixed_t[at:at + HEAD_DIM, part * half:(part + 1) * half] = (
            o[:HEAD_DIM] / o[HEAD_DIM:HEAD_DIM + 1]).astype(BF16)

    def finish(part, rows):
        at = slice(part * rows, (part + 1) * rows)
        after = x[at, :] + mm(mixed_t[:, at].T, w_out[...])
        normal = normed(after, gain[1:2, :])
        hidden = w_up.shape[1]
        chunk = 512
        total = after
        up = mm(normal, w_up[:, :chunk])
        for at in range(0, hidden, chunk):
            following = mm(normal, w_up[:, at + chunk:at + 2 * chunk]) if at + chunk < hidden else None
            total = total + mm(gelu(up), w_down[at:at + chunk, :])
            up = following
        emit(part, total)

    steps = [(part, i) for part in range(PATCH // half) for i in range(heads)]
    lead, lag = 2, 2
    score = {n: scores(steps[n]) for n in range(lead)}
    weights = {}
    for n in range(len(steps) + lag):
        if n + lead < len(steps):
            score[n + lead] = scores(steps[n + lead])
        if n < len(steps):
            weights[n] = raised(score.pop(n))
        if n >= lag:
            mix(steps[n - lag], weights.pop(n - lag))
            if parts > 1 and n - lag + 1 == heads:
                finish(0, half)
    if parts > 1:
        finish(1, half)
    else:
        finish(0, PATCH)


ORDER = (1, 4, 3, 12, 5, 15, 13, 7, 2, 8, 6, 9, 11, 14, 10)


def kernel(n_scene, n_seg, order_ref, target_ref, gain_ref, image_row_ref,
           image_hbm, weight_hbm, points_hbm, in_hbm, out_hbm, up_hbm, down_hbm, result_ref,
           image, image_weight, points, w_in, w_out, w_up, w_down,
           table, targets, inverse_v, inverse, hot, x, query, key, value_t, mixed_t,
           send1, recv1, send2, recv2,
           wsem, psem, isem, asend, arecv, fsend, frecv, tsend, trecv, ssem1, rsem1, ssem2, rsem2):
    scene = lax.axis_index("scene")
    me = lax.axis_index("seg")
    blocks, size, width = points.shape
    per = PATCH // size
    patches = blocks // per
    columns = width // COLS
    count = image.shape[0]
    side = 4
    core = scene % 2
    level = scene // 2
    chips = n_scene // 2
    other = level * 2 + 1 - core

    def peer(k):
        return (me // side + k // side) % side * side + (me + k) % side

    first = [pltpu.make_async_copy(image_hbm, image, isem.at[0]),
             pltpu.make_async_copy(weight_hbm, image_weight, isem.at[1])]
    for load in first:
        load.start()
    barrier = pltpu.get_barrier_semaphore()
    for k in range(1, chips):
        pl.semaphore_signal(barrier, inc=1, device_id=((level + k) % chips * 2 + core, me), device_id_type=MESH)
    pl.semaphore_signal(barrier, inc=1, device_id=(other, me), device_id_type=MESH)
    for k in range(1, n_seg):
        pl.semaphore_signal(barrier, inc=1, device_id=(scene, peer(k)), device_id_type=MESH)

    load_points = pltpu.make_async_copy(points_hbm, points, psem.at[0])
    loads = [
        [pltpu.make_async_copy(src.at[layer], dst.at[layer], wsem.at[layer, j])
         for j, (src, dst) in enumerate(((in_hbm, w_in), (out_hbm, w_out), (up_hbm, w_up), (down_hbm, w_down)))]
        for layer in range(2)
    ]

    sublane = lax.broadcasted_iota(I32, (16, 128), 0)
    column = jnp.full((16, 128), -1, I32)
    for j in range(blocks):
        column = jnp.where(sublane == j, target_ref[j], column)
    targets[me] = column
    for load in first:
        load.wait()
    table[scene] = mm(image[...], image_weight[...]).astype(BF16)
    pl.semaphore_wait(barrier, chips + n_seg - 1)

    def across(k):
        return pltpu.make_async_remote_copy(
            table.at[scene], table.at[scene], asend.at[k], arecv.at[k],
            device_id=((level + k) % chips * 2 + core, me), device_id_type=MESH)

    def forward(k):
        held = (level + chips - k) % chips * 2 + core
        return pltpu.make_async_remote_copy(
            table.at[held], table.at[held], fsend.at[k], frecv.at[k],
            device_id=(other, me), device_id_type=MESH)

    def tell(k):
        return pltpu.make_async_remote_copy(
            targets.at[me], targets.at[me], tsend.at[k], trecv.at[k],
            device_id=(scene, peer(k)), device_id_type=MESH)

    hops = [k for k in (1, chips - 1, 2)]
    for k in hops:
        across(k).start()
    forward(0).start()
    for k in ORDER:
        tell(k).start()
    for load in [load_points] + loads[0] + loads[1]:
        load.start()
    for k in hops[:2]:
        across(k).wait_recv()
        forward(k).start()
    for k in ORDER:
        tell(k).wait_recv()
    base = scene * (n_seg * blocks)
    lane = lax.broadcasted_iota(I32, (16, 128), 1)
    within = sublane // per * (n_seg * per) + sublane % per
    for part in range(2):
        total = jnp.zeros((16, 128), I32)
        for source in range(n_seg):
            hit = targets[source] == lane + (base + part * 128)
            total = total + jnp.where(hit, within + source * per, 0)
        summed = total[:8] + total[8:]
        for step in (4, 2, 1):
            summed = summed[:step] + summed[step:]
        summed = jnp.minimum(summed, n_seg * blocks - 1)
        inverse_v[part * 8:(part + 1) * 8, :] = jnp.broadcast_to(summed, (8, 128))
    to_scalars = pltpu.make_async_copy(inverse_v, inverse, isem.at[2])
    to_scalars.start()
    across(2).wait_recv()
    forward(2).start()
    row = image_row_ref[...]
    entry = lax.shift_right_logical(row, 11) * count + (row & (count - 1))
    entry = jnp.concatenate([entry, jnp.zeros((16 - blocks, size), I32)], axis=0).astype(F32).T
    pick = lax.broadcasted_iota(I32, (size, 16), 1)
    rows = lax.broadcasted_iota(I32, (size, n_scene * count), 1)
    for b in range(blocks):
        block = lax.rem(order_ref[b], blocks)
        mine = jnp.sum(jnp.where(pick == block, entry, 0.0), axis=1, keepdims=True).astype(I32)
        hot[b * size:(b + 1) * size, :] = jnp.where(rows == mine, 1.0, 0.0).astype(BF16)
    load_points.wait()
    for load in loads[0]:
        load.wait()
    for k in range(chips):
        forward(k).wait_recv()
    to_scalars.wait()

    def piece(ref, patch, device):
        return ref.at[pl.ds((patch * n_seg + device) * per, per)]

    def copy1(patch, part, k):
        ranks = per // 2
        there = pl.ds((patch * n_seg + peer(k)) * per + part * ranks, ranks)
        here = pl.ds((patch * n_seg + me) * per + part * ranks, ranks)
        return pltpu.make_async_remote_copy(
            send1.at[there], recv1.at[here], ssem1.at[patch * 2 + part, k], rsem1.at[patch * 2 + part, k],
            device_id=(scene, peer(k)), device_id_type=MESH)

    def copy2(patch, k):
        return pltpu.make_async_remote_copy(
            piece(send2, patch, peer(k)), piece(recv2, patch, me), ssem2.at[patch, k], rsem2.at[patch, k],
            device_id=(scene, peer(k)), device_id_type=MESH)

    def compute(layer, parts, emit):
        layer_patch(x, gain_ref.at[layer], w_in.at[layer], w_out.at[layer], w_up.at[layer],
                    w_down.at[layer], query, key, value_t, mixed_t, parts, emit)

    def first_patch(patch, parts):
        at = pl.ds(patch * PATCH, PATCH)
        x[...] = mm(hot[at, :], table[...].reshape(n_scene * count, width))
        for b in range(per):
            block = lax.rem(order_ref[patch * per + b], blocks)
            x[b * size:(b + 1) * size, :] += points[block].astype(F32)

        def emit(part, result):
            out = result.astype(BF16)
            for j in range(per // parts):
                b = part * (per // parts) + j
                for r in range(size // ROWS):
                    for c in range(columns):
                        send1[(patch * n_seg + r * columns + c) * per + b] = (
                            out[j * size + r * ROWS:j * size + (r + 1) * ROWS, c * COLS:(c + 1) * COLS])
            for half in range(2 // parts):
                for k in ORDER:
                    copy1(patch, part + half, k).start()

        compute(0, parts, emit)
        for b in range(per):
            recv1[(patch * n_seg + me) * per + b] = send1[(patch * n_seg + me) * per + b]

    def whole_patch(patch, carry):
        first_patch(patch, 1)
        return carry

    lax.fori_loop(0, patches - 1, whole_patch, 0)
    first_patch(patches - 1, 2)
    for patch in range(patches):
        for part in range(2):
            for k in ORDER:
                copy1(patch, part, k).wait_recv()

    def send_patch(patch):
        for k in ORDER:
            copy2(patch, k).start()

    for patch in range(patches):
        def fill(device, carry):
            for s in range(per):
                t = device * blocks + patch * per + s
                send2[(patch * n_seg + device) * per + s] = recv1[inverse[t // 128 * 8, t % 128]]
            return carry

        if patch == 0:
            for k in ORDER:
                fill(peer(k), 0)
                copy2(0, k).start()
            fill(me, 0)
        else:
            lax.fori_loop(0, n_seg, fill, 0)
        for s in range(per):
            recv2[(patch * n_seg + me) * per + s] = send2[(patch * n_seg + me) * per + s]
    for load in loads[1]:
        load.wait()

    def second_patch(patch, carry):
        for k in ORDER:
            copy2(patch, k).wait_recv()

        @pl.when(patch + 1 < patches)
        def _():
            send_patch(patch + 1)

        for s in range(per):
            for r in range(size // ROWS):
                for c in range(columns):
                    x[s * size + r * ROWS:s * size + (r + 1) * ROWS, c * COLS:(c + 1) * COLS] = (
                        recv2[(patch * n_seg + r * columns + c) * per + s].astype(F32))

        def emit(part, result):
            result_ref[pl.ds(patch * PATCH, PATCH), :] = result.astype(BF16)

        compute(1, 1, emit)
        return carry

    lax.fori_loop(0, patches, second_patch, 0)
    for k in hops:
        across(k).wait_send()
    for k in range(chips):
        forward(k).wait_send()
    for k in ORDER:
        tell(k).wait_send()
    for patch in range(patches):
        for k in ORDER:
            copy1(patch, 0, k).wait_send()
            copy1(patch, 1, k).wait_send()
            copy2(patch, k).wait_send()


def local(n_scene, n_seg, points, zorder, image, image_row, image_weight, norm_gain, in_weight, out_weight,
          up_weight, down_weight, hilbert_target):
    length, width = points.shape
    blocks = zorder.shape[0]
    size = length // blocks
    patches = length // PATCH
    count = image.shape[0]
    chips = n_scene // 2
    whole = pl.BlockSpec(memory_space=pltpu.VMEM)
    scalar = pl.BlockSpec(memory_space=pltpu.SMEM)
    hbm = pl.BlockSpec(memory_space=pl.ANY)
    pieces = (length // ROWS * (width // COLS), ROWS, COLS)
    dma = pltpu.SemaphoreType.DMA
    return pl.pallas_call(
        functools.partial(kernel, n_scene, n_seg),
        out_shape=pltpu.VMEM((length, width), BF16),
        in_specs=[scalar, scalar, whole, whole] + [hbm] * 7,
        out_specs=whole,
        scratch_shapes=[
            pltpu.VMEM(image.shape, BF16),
            pltpu.VMEM(image_weight.shape, BF16),
            pltpu.VMEM((blocks, size, width), BF16),
            pltpu.VMEM(in_weight.shape, BF16),
            pltpu.VMEM(out_weight.shape, BF16),
            pltpu.VMEM(up_weight.shape, BF16),
            pltpu.VMEM(down_weight.shape, BF16),
            pltpu.VMEM((n_scene, count, width), BF16),
            pltpu.VMEM((n_seg, 16, 128), I32),
            pltpu.VMEM((16, 128), I32),
            pltpu.SMEM((16, 128), I32),
            pltpu.VMEM((length, n_scene * count), BF16),
            pltpu.VMEM((PATCH, width), F32),
            pltpu.VMEM((PATCH, width), BF16),
            pltpu.VMEM((PATCH, width), BF16),
            pltpu.VMEM((width, PATCH), BF16),
            pltpu.VMEM((width, PATCH), BF16),
            pltpu.VMEM(pieces, BF16),
            pltpu.VMEM(pieces, BF16),
            pltpu.VMEM(pieces, BF16),
            pltpu.VMEM(pieces, BF16),
            dma((2, 4)),
            dma((1,)),
            dma((3,)),
            dma((chips,)),
            dma((chips,)),
            dma((chips,)),
            dma((chips,)),
            dma((n_seg,)),
            dma((n_seg,)),
            dma((patches * 2, n_seg)),
            dma((patches * 2, n_seg)),
            dma((patches, n_seg)),
            dma((patches, n_seg)),
        ],
        compiler_params=pltpu.CompilerParams(
            collective_id=0, has_side_effects=True, vmem_limit_bytes=VMEM_LIMIT),
    )(zorder, hilbert_target, norm_gain, image_row.reshape(blocks, size), image, image_weight,
      points.reshape(blocks, size, width), in_weight, out_weight, up_weight, down_weight)


def solution(mesh):
    placed = (
        P(("scene", "seg"), None),
        P(("scene", "seg")),
        P(("scene", "seg"), None),
        P(("scene", "seg")),
        P(),
        P(),
        P(),
        P(),
        P(),
        P(),
        P(("scene", "seg")),
    )
    return jax.shard_map(
        functools.partial(local, mesh.shape["scene"], mesh.shape["seg"]),
        mesh=mesh, in_specs=placed, out_specs=P(("scene", "seg"), None), check_vma=False)
```
